128 devices in a mesh: grp: 4 (over y), loc: 32 (over x, z, core).
Axes of the slice: x: 4, y: 4, z: 4, core: 2. Of those that a mesh axis runs over, the one named last changes fastest.
Arguments:
- hidden: bfloat16 [16384, 4096], P(('grp', 'loc')), may hold values from -6 to 6
- norm_gain: bfloat16 [4096], replicated, may hold values from 0.25 to 1.75
- w_gate: bfloat16 [32, 4096, 3072], P('loc', None, 'grp'), may hold values from -0.09375 to 0.09375
- w_up: bfloat16 [32, 4096, 3072], P('loc', None, 'grp'), may hold values from -0.09375 to 0.09375
- w_down: bfloat16 [32, 3072, 4096], P('loc', 'grp'), may hold values from -0.109375 to 0.109375
- routes: int32 [16384, 2], P(('grp', 'loc')), may hold values from 0 to 31, all different within a row; in each aligned block of 128 rows (0 to 127, 128 to 255, ...) at most 12 rows name the same one
- gate_weights: bfloat16 [16384, 2], P(('grp', 'loc')), may hold values from 0.049804688 to 1
Outputs:
- moe_out: bfloat16 [16384, 4096], P(('grp', 'loc'))
The draws below stay inside these ranges and needn't reach their ends.
Inputs may be any that keep to these rules, and one draw needn't show every extreme that they name: `routes`: among the 128 rows of one device no expert is named by more than 12 rows, a bound that some block reaches in some devices' rows. A row names 2 different experts.
All inputs are finite; a program needn't handle non-finite values.
Results may differ from the reference program's by a relative error of at most 0.015.
Values may be sent and summed in bfloat16 or wider, within the bound.
No kernel may reach another device: no remote copies, remote signals or barrier semaphores. Data moves between devices by JAX's collectives and lax.ppermute only.
A program may use at most 128 MiB of HBM per device.

```python
import math
import jax
import jax.numpy as jnp
import numpy as np
from jax import lax

D = 4096
FF = 3072
EXPERTS = 32
TOP = 2
TOK_DEV = 128
CAP = 12
FF_DEV = 768
TOKENS = 16384
N_GRP = 4


def block_scale(own_key, extent, shards, low, top_value):
    level = 1.0
    for axis_at, blocks in shards:
        draws = jax.random.uniform(jax.random.fold_in(jax.random.fold_in(own_key, 6), axis_at), (blocks,), jnp.float32, low / len(shards), top_value / len(shards))
        level = level * jnp.repeat(jnp.exp(draws), extent[axis_at] // blocks).reshape((-1,) + (1,) * (len(extent) - 1 - axis_at))
    return level


def deal_out(stream_key, own, number, rows, number_of, top, most, skew):
    ranking = jax.random.permutation(stream_key, number_of)
    packed, common = shares(number_of, rows * top, most, skew, True), shares(number_of, rows * top, most, skew, False)
    places = jnp.arange(number_of)

    def named(tallies, turn):
        used = int((tallies > 0).sum())
        fixed = max(1, used // 4)
        shifted = fixed + (places - fixed + turn * (used - fixed)) % max(1, number_of - fixed)
        return jnp.zeros((number_of,), jnp.int32).at[ranking[jnp.where(places < fixed, places, shifted)]].set(jnp.asarray(tallies, jnp.int32))

    tallies = jnp.where(number % 4 == 0, named(packed, number // 4), named(common, number - number // 4 - 1))
    mixed = jax.random.permutation(jax.random.fold_in(own, 3), number_of)
    giver, receiver = mixed[0:number_of // 2 * 2:2], mixed[1:number_of // 2 * 2:2]
    room = jnp.minimum(tallies[giver] - 1, most - tallies[receiver]) // 2
    room = jnp.where((giver == ranking[0]) | (receiver == ranking[0]) | (tallies[receiver] == 0), 0, jnp.maximum(room, 0))
    shifted = jax.random.randint(jax.random.fold_in(own, 4), (number_of // 2,), 0, 1 << 20) % (room + 1)
    tallies = tallies.at[giver].add(-shifted).at[receiver].add(shifted)
    items = jnp.searchsorted(jnp.cumsum(tallies), jnp.arange(rows * top), side="right").astype(jnp.int32)
    grid = items.reshape(top, rows).T
    grid = grid[jax.random.permutation(jax.random.fold_in(own, 1), rows)]
    turn = jax.random.randint(jax.random.fold_in(own, 2), (rows, 1), 0, top)
    return jnp.take_along_axis(grid, (jnp.arange(top)[None, :] + turn) % top, axis=1)


def shares(amount, total, most, lean, full):
    loads = [(1 << 20) // math.isqrt(rank ** lean) + 1 for rank in range(1, amount + 1)]
    largest = most if full else min(most, max(-(-total // amount), total * loads[0] // sum(loads)))
    least = 1 if total - largest >= amount - 1 else 0
    counts, surplus = [largest] + [least] * (amount - 1), total - largest - least * (amount - 1)
    while surplus > 0:
        candidates = [i for i in range(1, amount) if counts[i] < largest] or [i for i in range(1, amount) if counts[i] < most]
        mass, budget = sum([loads[i] for i in candidates]), surplus
        for i in candidates:
            extra = min(most - counts[i], max(1, budget * loads[i] // mass), surplus)
            counts[i] = counts[i] + extra
            surplus = surplus - extra
    return np.array(counts)


def bell_draw(stream_key, shape, spread, reach, pieces=(), held_as=jnp.bfloat16):
    result = spread * jax.random.normal(stream_key, shape, jnp.float32)
    if pieces:
        result = result * block_scale(stream_key, shape, pieces, -0.22, 0.18)
    return jnp.clip(result, -reach, reach).astype(held_as)


def setup_inputs(seed: int = 0) -> dict:
    key_list = jax.random.split(jax.random.key(seed), 8)
    hidden = bell_draw(key_list[0], (TOKENS, D), 1.0, 6.0, ((0, 128),))
    norm_gain = jnp.clip(1.0 + 0.15 * jax.random.normal(key_list[1], (D,), jnp.float32), 0.25, 1.75).astype(jnp.bfloat16)
    w_gate = bell_draw(key_list[2], (EXPERTS, D, FF), D ** -0.5, 0.09375, ((0, 32), (2, 4)))
    w_up = bell_draw(key_list[3], (EXPERTS, D, FF), D ** -0.5, 0.09375, ((0, 32), (2, 4)))
    w_down = bell_draw(key_list[4], (EXPERTS, FF, D), FF ** -0.5, 0.109375, ((0, 32), (1, 4)))
    routes_keys = jax.random.split(jax.random.fold_in(key_list[5], 1), TOKENS // TOK_DEV)
    routes_turns = jax.random.permutation(jax.random.fold_in(key_list[5], 3), TOKENS // TOK_DEV)
    routes = jax.vmap(lambda own, number: deal_out(jax.random.fold_in(key_list[5], 2), own, number, TOK_DEV, EXPERTS, TOP, CAP, 2))(routes_keys, routes_turns).reshape((TOKENS, TOP))
    gate_weights = jnp.clip(jnp.exp(math.log(1.0) - 2.9996462 * jax.random.uniform(key_list[6], (TOKENS, TOP), jnp.float32) ** block_scale(key_list[6], (TOKENS, TOP), ((0, 128),), -0.2, 0.2)), 0.049804688, 1.0).astype(jnp.bfloat16)
    return {"hidden": hidden, "norm_gain": norm_gain, "w_gate": w_gate, "w_up": w_up, "w_down": w_down, "routes": routes, "gate_weights": gate_weights}


def reference(hidden, norm_gain, w_gate, w_up, w_down, routes, gate_weights):
    values = hidden.astype(jnp.float32)
    scale = lax.rsqrt(lax.optimization_barrier(jnp.mean(values * values, axis=-1, keepdims=True)) + 1e-06)
    normed = (values * scale * norm_gain.astype(jnp.float32)).astype(jnp.bfloat16)
    blocks = TOKENS // TOK_DEV
    chosen = routes.reshape(blocks, TOK_DEV * TOP)
    one_hot = (chosen[:, :, None] == jnp.arange(EXPERTS, dtype=jnp.int32)).astype(jnp.int32)
    slots = lax.optimization_barrier(jnp.sum((jnp.cumsum(one_hot, axis=1) - one_hot) * one_hot, axis=-1)).astype(jnp.int32)
    per_expert = blocks * CAP
    positions = (chosen * per_expert + jnp.arange(blocks, dtype=jnp.int32)[:, None] * CAP + slots).reshape(-1).astype(jnp.int32)
    owners = jnp.repeat(jnp.arange(TOKENS, dtype=jnp.int32), TOP)
    table = jnp.zeros((EXPERTS * per_expert,), jnp.int32).at[positions].set(owners)
    factors = jnp.zeros((EXPERTS * per_expert,), jnp.float32).at[positions].set(gate_weights.reshape(-1).astype(jnp.float32))

    def expert_step(combined, inputs):
        members, weights, gate_mat, up_mat, down_mat = inputs
        selected = jnp.take(normed, members, axis=0)
        gate = jnp.dot(selected, gate_mat, preferred_element_type=jnp.float32)
        up = jnp.dot(selected, up_mat, preferred_element_type=jnp.float32)
        units = (jax.nn.silu(gate) * up).astype(jnp.bfloat16)
        quarters = units.reshape(per_expert, N_GRP, FF_DEV).astype(jnp.float32)
        down = down_mat.reshape(N_GRP, FF_DEV, D).astype(jnp.float32)
        parts = jnp.einsum('rqf,qfd->rqd', quarters, down)
        rounded = lax.optimization_barrier(parts.astype(jnp.bfloat16)).astype(jnp.float32)
        summed = lax.optimization_barrier(jnp.sum(rounded, axis=1))
        combined = combined.at[members].add(summed * weights[:, None])
        return (combined, None)
    combined, _ = lax.scan(expert_step, jnp.zeros((TOKENS, D), jnp.float32), (table.reshape(EXPERTS, per_expert), factors.reshape(EXPERTS, per_expert), w_gate, w_up, w_down))
    return combined.astype(jnp.bfloat16)
```

```python
import jax
import jax.numpy as jnp
from jax import lax
from jax.sharding import PartitionSpec as P

EXPERTS = 32
CAP = 12
CORES = 2
SPLIT = 1664
INFO = 128


def row_match(info, core, chips):
    groups, cores, tokens, _ = info.shape
    rows = chips * cores * CAP
    expert = info[..., 0:2].astype(jnp.int32)
    slot = info[..., 2:4].astype(jnp.int32)
    weight = info[..., 4:6]
    side = jnp.arange(cores, dtype=jnp.int32)[None, :, None, None]
    target = (expert // CORES) * (cores * CAP) + side * CAP + slot
    target = jnp.where(expert % CORES == core, target, -1)
    target = target.reshape(groups, 1, cores * tokens, 2)
    weight = weight.reshape(groups, 1, cores * tokens, 2)
    hit = target == jnp.arange(rows, dtype=jnp.int32)[None, :, None, None]
    picker = jnp.any(hit, axis=-1).astype(jnp.bfloat16)
    mixing = jnp.sum(jnp.where(hit, weight, jnp.zeros_like(weight)), axis=-1)
    return picker, mixing


def on_device(hidden, norm_gain, w_gate, w_up, w_down, routes, gate_weights):
    tokens_here, width = hidden.shape
    chips = EXPERTS // CORES
    n_grp = lax.axis_size("grp")
    loc = lax.axis_index("loc")
    grp = lax.axis_index("grp")
    core = loc % CORES
    plane = [[CORES * i + c for i in range(chips)] for c in range(CORES)]
    swap = [(i, i ^ 1) for i in range(EXPERTS)]
    block = CORES * CAP

    def exchange(rows):
        out = lax.all_to_all(
            rows.reshape(chips, block, -1), "loc", 0, 0, tiled=True, axis_index_groups=plane
        )
        return out.reshape(chips * block, -1)

    values = hidden.astype(jnp.float32)
    scale = lax.rsqrt(jnp.mean(values * values, axis=-1, keepdims=True) + 1e-06)
    normed = (values * scale * norm_gain.astype(jnp.float32)).astype(jnp.bfloat16)
    chosen = routes.reshape(-1)
    same = chosen[:, None] == chosen[None, :]
    before = jnp.arange(chosen.shape[0])[None, :] < jnp.arange(chosen.shape[0])[:, None]
    slots = jnp.sum((same & before).astype(jnp.int32), axis=1).reshape(routes.shape)
    info = jnp.concatenate(
        [routes.astype(jnp.bfloat16), slots.astype(jnp.bfloat16), gate_weights], axis=1
    )
    info = jnp.pad(info, ((0, 0), (0, INFO - info.shape[1])))

    early = jnp.concatenate([normed[:, :SPLIT], info], axis=1)
    late = jnp.concatenate([normed[:, SPLIT:], info], axis=1)
    early_all = lax.all_gather(early, "grp", axis=0, tiled=True)
    late_both = jnp.stack([late, lax.ppermute(late, "loc", swap)])
    early_peer = lax.ppermute(early_all, "loc", swap)
    early_both = jnp.stack(
        [early_all.reshape(n_grp, tokens_here, -1), early_peer.reshape(n_grp, tokens_here, -1)],
        axis=1,
    )

    pick_own, mix_own = row_match(late_both[None, :, :, -INFO:], core, chips)
    pick_all, mix_all = row_match(early_both[..., -INFO:], core, chips)

    late_rows = jnp.dot(
        pick_own[0],
        late_both[..., :-INFO].reshape(CORES * tokens_here, -1),
        preferred_element_type=jnp.float32,
    ).astype(jnp.bfloat16)
    late_in = lax.all_gather(exchange(late_rows), "grp", axis=0, tiled=False)
    early_rows = jnp.einsum(
        "gpt,gtd->gpd",
        pick_all,
        early_both[..., :-INFO].reshape(n_grp, CORES * tokens_here, -1),
        preferred_element_type=jnp.float32,
    ).astype(jnp.bfloat16)
    early_in = [exchange(early_rows[g]) for g in range(n_grp)]

    def dot(a, b):
        return jnp.dot(a, b, preferred_element_type=jnp.float32)

    units = []
    for g in range(n_grp):
        gate = dot(early_in[g], w_gate[0, :SPLIT]) + dot(late_in[g], w_gate[0, SPLIT:])
        up = dot(early_in[g], w_up[0, :SPLIT]) + dot(late_in[g], w_up[0, SPLIT:])
        units.append((jax.nn.silu(gate) * up).astype(jnp.bfloat16))

    late_part = jnp.concatenate([dot(u, w_down[0, :, SPLIT:]).astype(jnp.bfloat16) for u in units])
    late_sum = lax.psum_scatter(late_part, "grp", scatter_dimension=0, tiled=True)
    early_back = [exchange(dot(u, w_down[0, :, :SPLIT]).astype(jnp.bfloat16)) for u in units]
    late_back = exchange(late_sum)

    early_mix = [
        lax.dot_general(
            mix_all[g], early_back[g], (((0,), (0,)), ((), ())), preferred_element_type=jnp.float32
        ).reshape(CORES, tokens_here, -1)
        for g in range(n_grp)
    ]
    early_theirs = lax.ppermute(
        jnp.concatenate([m[1] for m in early_mix]).astype(jnp.bfloat16), "loc", swap
    )
    early_mine = jnp.concatenate([m[0] for m in early_mix]) + early_theirs.astype(jnp.float32)
    early_out = lax.psum_scatter(
        early_mine.astype(jnp.bfloat16), "grp", scatter_dimension=0, tiled=True
    )
    late_mix = lax.dot_general(
        mix_own[0], late_back, (((0,), (0,)), ((), ())), preferred_element_type=jnp.float32
    ).reshape(CORES, tokens_here, -1)
    late_theirs = lax.ppermute(late_mix[1].astype(jnp.bfloat16), "loc", swap)
    late_out = (late_mix[0] + late_theirs.astype(jnp.float32)).astype(jnp.bfloat16)
    return jnp.concatenate([early_out, late_out], axis=1)


def solution(mesh):
    placed = (
        P(("grp", "loc"), None),
        P(),
        P("loc", None, "grp"),
        P("loc", None, "grp"),
        P("loc", "grp", None),
        P(("grp", "loc"), None),
        P(("grp", "loc"), None),
    )
    return jax.shard_map(
        on_device, mesh=mesh, in_specs=placed, out_specs=P(("grp", "loc"), None), check_vma=False
    )
```

```python
import functools
import jax
import jax.numpy as jnp
from jax import lax
from jax.experimental import pallas as pl
from jax.experimental.pallas import tpu as pltpu
from jax.sharding import PartitionSpec as P

EXPERTS = 32
CAP = 12
CORES = 2
INFO = 128
SPLIT = 1536
HALF = 1280
TILE = 256


BF16 = jnp.bfloat16
F32 = jnp.float32
ROWS = EXPERTS * CAP
WHOLE = pl.BlockSpec(memory_space=pltpu.VMEM)
SCALAR = pl.BlockSpec(memory_space=pltpu.SMEM)


def dot(a, b):
    return jnp.dot(a, b, preferred_element_type=F32)


def dot_t(a, b):
    return lax.dot_general(a, b, (((0,), (0,)), ((), ())), preferred_element_type=F32)


def tiles(width):
    step = 512 if width % 512 == 0 else 256
    return [slice(at, at + step) for at in range(0, width, step)]


def columns(rows, width, index):
    return pl.BlockSpec((rows, width), lambda i: (0, index))


def cost(flops, size):
    return pl.CostEstimate(flops=flops, bytes_accessed=size, transcendentals=0)


def prepare_kernel(hidden, gain, routes, weights, out, sent):
    tokens, width = hidden.shape
    values = hidden[...].astype(F32)
    scale = lax.rsqrt(jnp.mean(values * values, axis=-1, keepdims=True) + 1e-06)
    out[:, :width] = (values * scale * gain[...].astype(F32)).astype(BF16)
    row = lax.broadcasted_iota(jnp.int32, (tokens, tokens), 0)
    col = lax.broadcasted_iota(jnp.int32, (tokens, tokens), 1)

    def upright(line):
        return jnp.sum(jnp.where(row == col, line.astype(F32), 0.0), axis=-1, keepdims=True)

    experts = [upright(routes[k:k + 1, :]) for k in range(2)]
    factors = [upright(weights[k:k + 1, :]) for k in range(2)]
    lane = lax.broadcasted_iota(jnp.int32, (tokens, INFO), 1)
    hits = [lane == e.astype(jnp.int32) for e in experts]
    named = (hits[0] | hits[1]).astype(F32).astype(BF16)
    earlier = dot((col < row).astype(F32).astype(BF16), named)
    info = jnp.zeros((tokens, INFO), F32)
    for k in range(2):
        slot = jnp.sum(jnp.where(hits[k], earlier, 0.0), axis=-1, keepdims=True)
        info = jnp.where(lane == k, experts[k], info)
        info = jnp.where(lane == 2 + k, slot, info)
        info = jnp.where(lane == 4 + k, factors[k], info)
    out[:, width:] = info.astype(BF16)
    sent[:, :SPLIT] = out[:, :SPLIT]
    sent[:, SPLIT:] = info.astype(BF16)


def prepare(hidden, gain, routes, weights):
    tokens, width = hidden.shape
    return pl.pallas_call(
        prepare_kernel,
        out_shape=[
            jax.ShapeDtypeStruct((tokens, width + INFO), BF16),
            jax.ShapeDtypeStruct((tokens, SPLIT + INFO), BF16),
        ],
        in_specs=[WHOLE] * 4,
        out_specs=[WHOLE] * 2,
        compiler_params=pltpu.CompilerParams(vmem_limit_bytes=16 * 1024 * 1024),
        cost_estimate=cost(0, 4 * tokens * width),
    )(hidden, gain.reshape(1, -1), routes.T, weights.T)


def places(info, side, core):
    info = info.astype(F32)
    row = lax.broadcasted_iota(jnp.int32, (info.shape[0], ROWS), 1)
    held = jnp.zeros(row.shape, F32)
    weight = jnp.zeros(row.shape, F32)
    for k in range(2):
        expert = info[:, k:k + 1].astype(jnp.int32)
        slot = info[:, 2 + k:3 + k].astype(jnp.int32)
        target = (expert >> 1) * (CORES * CAP) + side * CAP + slot
        target = jnp.where((expert & 1) == core, target, -1)
        held = jnp.where(row == target, 1.0, held)
        weight = jnp.where(row == target, info[:, 4 + k:5 + k], weight)
    return held.astype(BF16), weight.astype(BF16)


def gather_kernel(n_groups, first, cuts, core, *refs):
    outs = refs[2 * n_groups:]
    width = sum(cuts)
    at = 0
    for g in range(n_groups):
        mine, theirs = refs[2 * g:2 * g + 2]
        last = mine.shape[1] - INFO
        picks = [places(a[:, last:], side, core[0])[0] for side, a in enumerate((mine, theirs))]
        begin = first
        for i, cut in enumerate(cuts):
            for part in tiles(cut):
                source = slice(begin + part.start, begin + part.stop)
                rows = dot_t(picks[0], mine[:, source]) + dot_t(picks[1], theirs[:, source])
                out = outs[i]
                out[:, g * cut + part.start:g * cut + part.stop] = rows.astype(BF16)
            begin += cut


def gather(core, groups, first, cuts):
    flat = [a for pair in groups for a in pair]
    n_groups = len(groups)
    return pl.pallas_call(
        functools.partial(gather_kernel, n_groups, first, cuts),
        out_shape=[jax.ShapeDtypeStruct((ROWS, cut * n_groups), BF16) for cut in cuts],
        in_specs=[SCALAR] + [WHOLE] * len(flat),
        out_specs=[WHOLE] * len(cuts),
        compiler_params=pltpu.CompilerParams(vmem_limit_bytes=24 * 1024 * 1024),
        cost_estimate=cost(0, n_groups * ROWS * sum(cuts) * 4),
    )(core, *flat)


def mix_kernel(n_groups, core, *refs):
    back, mine_out, theirs_out = refs[2 * n_groups:]
    width = back.shape[1] // n_groups
    for g in range(n_groups):
        for side, out in enumerate((mine_out, theirs_out)):
            info = refs[2 * g + side]
            tokens = info.shape[0]
            weight = places(info[...], side, core[0])[1]
            for part in tiles(width):
                source = slice(g * width + part.start, g * width + part.stop)
                out[g * tokens:(g + 1) * tokens, part] = dot(weight, back[:, source]).astype(out.dtype)


def mix(core, groups, back):
    n_groups = len(groups)
    tokens = groups[0][0].shape[0]
    width = back.shape[1] // n_groups
    flat = [a for pair in groups for a in pair]
    specs = [columns(tokens, INFO, a.shape[1] // INFO - 1) for a in flat]
    return pl.pallas_call(
        functools.partial(mix_kernel, n_groups),
        out_shape=[
            jax.ShapeDtypeStruct((n_groups * tokens, width), F32),
            jax.ShapeDtypeStruct((n_groups * tokens, width), BF16),
        ],
        grid=(1,),
        in_specs=[SCALAR] + specs + [WHOLE],
        out_specs=[WHOLE] * 2,
        compiler_params=pltpu.CompilerParams(vmem_limit_bytes=24 * 1024 * 1024),
        cost_estimate=cost(0, ROWS * back.shape[1] * 4),
    )(core, *flat, back)


def expert_kernel(index, carried, n_out, *refs):
    early_hbm, low, high, gate_hbm, up_hbm, down_hbm = refs[:6]
    refs = refs[6:]
    if carried:
        carry, refs = refs[0], refs[1:]
    outs = refs[:n_out]
    gate_w, up_w, down_w, units, gate_sum, up_sum, early, sems = refs[n_out:]
    depth = early.shape[1]
    early_copy = pltpu.make_async_copy(
        early_hbm.at[:, pl.ds(index * depth, depth)], early, sems.at[5]
    )
    early_copy.start()
    copies = []
    for i, part in enumerate((pl.ds(0, depth), pl.ds(depth, gate_w.shape[0] - depth))):
        copies.append((
            pltpu.make_async_copy(gate_hbm.at[0, part], gate_w.at[part], sems.at[2 * i]),
            pltpu.make_async_copy(up_hbm.at[0, part], up_w.at[part], sems.at[2 * i + 1]),
        ))
    down_copy = pltpu.make_async_copy(down_hbm.at[0], down_w, sems.at[4])
    for pair in copies:
        for copy in pair:
            copy.start()
    down_copy.start()
    if carried:
        outs[0][:, :depth] = carry[...]
    early_copy.wait()
    for copy in copies[0]:
        copy.wait()
    for at in range(0, units.shape[1], TILE):
        cols = slice(at, at + TILE)
        gate_sum[:, cols] = dot(early[...], gate_w[:depth, cols])
        up_sum[:, cols] = dot(early[...], up_w[:depth, cols])
    for copy in copies[1]:
        copy.wait()
    middle = depth + low.shape[1]
    for at in range(0, units.shape[1], TILE):
        cols = slice(at, at + TILE)
        gate = dot(low[...], gate_w[depth:middle, cols]) + dot(high[...], gate_w[middle:, cols])
        gate += gate_sum[:, cols]
        up = dot(low[...], up_w[depth:middle, cols]) + dot(high[...], up_w[middle:, cols])
        up += up_sum[:, cols]
        units[:, cols] = (gate / (1.0 + jnp.exp(-gate)) * up).astype(BF16)
    down_copy.wait()
    order = ((1, depth), (2, middle), (0, 0))
    for i, begin in order:
        skip = depth if carried and i == 0 else 0
        for at in range(0, outs[i].shape[1] - skip, TILE):
            cols = slice(begin + at, begin + at + TILE)
            outs[i][:, skip + at:skip + at + TILE] = dot(units[...], down_w[:, cols]).astype(BF16)


def expert(early, low, high, weights, carry=None):
    early, index = early
    rows = low.shape[0]
    width, hidden_units = weights[0].shape[1:]
    left = pl.BlockSpec(memory_space=pl.ANY)
    carries = [] if carry is None else [carry]
    cuts = (SPLIT * (1 + len(carries)), low.shape[1], high.shape[1])
    return pl.pallas_call(
        functools.partial(expert_kernel, index, bool(carries), len(cuts)),
        out_shape=[jax.ShapeDtypeStruct((rows, cut), BF16) for cut in cuts],
        in_specs=[left] + [WHOLE] * 2 + [left] * 3 + [WHOLE] * len(carries),
        out_specs=[WHOLE] * len(cuts),
        scratch_shapes=[
            pltpu.VMEM((width, hidden_units), BF16),
            pltpu.VMEM((width, hidden_units), BF16),
            pltpu.VMEM((hidden_units, width), BF16),
            pltpu.VMEM((rows, hidden_units), BF16),
            pltpu.VMEM((rows, hidden_units), F32),
            pltpu.VMEM((rows, hidden_units), F32),
            pltpu.VMEM((rows, SPLIT), BF16),
            pltpu.SemaphoreType.DMA((6,)),
        ],
        compiler_params=pltpu.CompilerParams(vmem_limit_bytes=44 * 1024 * 1024),
        cost_estimate=pl.CostEstimate(
            flops=12 * rows * width * hidden_units,
            bytes_accessed=6 * width * hidden_units + 4 * rows * width,
            transcendentals=rows * hidden_units,
        ),
    )(early, low, high, *weights, *carries)


def on_device(hidden, norm_gain, w_gate, w_up, w_down, routes, gate_weights):
    tokens_here, width = hidden.shape
    chips = EXPERTS // CORES
    n_grp = lax.axis_size("grp")
    core = lax.axis_index("loc") % CORES
    core = core.astype(jnp.int32).reshape(1)
    plane = [[CORES * i + c for i in range(chips)] for c in range(CORES)]
    weights = (w_gate, w_up, w_down)

    def swap(rows):
        return lax.ppermute(rows, "loc", [(i, i ^ 1) for i in range(EXPERTS)])

    def shift(rows, way):
        return lax.ppermute(rows, "grp", [(i, (i + way) % n_grp) for i in range(n_grp)])

    turn = [None]

    def after(rows, other):
        return rows if other is None else lax.optimization_barrier((rows, other))[0]

    def exchange(rows, *others):
        for other in others:
            rows = after(rows, other)
        blocks = after(rows, turn[0]).reshape(chips, rows.shape[0] // chips, -1)
        out = lax.all_to_all(blocks, "loc", 0, 0, tiled=True, axis_index_groups=plane)
        turn[0] = out
        return out.reshape(rows.shape)

    def b16(a):
        return a.astype(BF16)

    def f32(a):
        return a.astype(F32)

    own, sent = prepare(hidden, norm_gain, routes, gate_weights)
    own_pair = (own, swap(own))
    far, near, next_ = shift(sent, 2), shift(sent, 1), shift(sent, -1)
    low_rows, high_rows = gather(core, [own_pair], SPLIT, (HALF, width - SPLIT - HALF))

    low_own = exchange(low_rows)
    low_near, low_next = shift(low_own, 1), shift(low_own, -1)
    far_pair = (far, swap(far))
    near_pair = (near, swap(near))
    next_pair = (next_, swap(next_))
    high_own = exchange(high_rows, far, near, next_)
    high_near, high_next = shift(high_own, 1), shift(high_own, -1)
    low_far, high_far = shift(low_near, 1), shift(high_next, -1)
    first_in = exchange(gather(core, [own_pair, far_pair], 0, (SPLIT,))[0], low_near, low_next)
    second_in = exchange(gather(core, [near_pair, next_pair], 0, (SPLIT,))[0], high_near, high_next)

    early_out, low_sum, high_sum = expert((first_in, 0), low_own, high_own, weights)
    first_out, low_part, high_part = expert((first_in, 1), low_far, high_far, weights, early_out)
    low_back, high_back = shift(low_part, -1), shift(high_part, 1)
    first_back = exchange(first_out)
    near_out, low_part, high_part = expert((second_in, 0), low_near, high_near, weights)
    second_out, low_part2, high_part2 = expert((second_in, 1), low_next, high_next, weights, near_out)
    second_back = exchange(second_out, low_back, high_back)
    high_sum = f32(high_sum) + f32(shift(high_part, -1))
    low_sum = f32(low_sum) + f32(shift(low_part2, 1))
    low_sum = b16(low_sum + f32(shift(b16(f32(low_part) + f32(low_back)), -1)))
    high_sum = b16(high_sum + f32(shift(b16(f32(high_part2) + f32(high_back)), 1)))

    mine, theirs = mix(core, [own_pair, far_pair], first_back)
    mine = mine + f32(swap(theirs))
    total = mine[:tokens_here] + f32(shift(b16(mine[tokens_here:]), 2))
    mine, theirs = mix(core, [near_pair, next_pair], second_back)
    mine = b16(mine + f32(swap(theirs)))
    total += f32(shift(mine[:tokens_here], -1)) + f32(shift(mine[tokens_here:], 1))
    out = [b16(total)]
    for part in (low_sum, high_sum):
        mine, theirs = mix(core, [own_pair], exchange(part))
        out.append(b16(mine + f32(swap(theirs))))
    return jnp.concatenate(out, axis=1)


def solution(mesh):
    placed = (
        P(("grp", "loc"), None),
        P(),
        P("loc", None, "grp"),
        P("loc", None, "grp"),
        P("loc", "grp", None),
        P(("grp", "loc"), None),
        P(("grp", "loc"), None),
    )
    return jax.shard_map(
        on_device, mesh=mesh, in_specs=placed, out_specs=P(("grp", "loc"), None), check_vma=False
    )
```

```python
import functools
import jax
import jax.numpy as jnp
from jax import lax
from jax.experimental import pallas as pl
from jax.experimental.pallas import tpu as pltpu
from jax.sharding import PartitionSpec as P

EXPERTS = 32
CAP = 12
CORES = 2
INFO = 128
SPLIT = 1536
HALF = 1280
TILE = 256


BF16 = jnp.bfloat16
F32 = jnp.float32
ROWS = EXPERTS * CAP
WHOLE = pl.BlockSpec(memory_space=pltpu.VMEM)
SCALAR = pl.BlockSpec(memory_space=pltpu.SMEM)


def dot(a, b):
    return jnp.dot(a, b, preferred_element_type=F32)


def dot_t(a, b):
    return lax.dot_general(a, b, (((0,), (0,)), ((), ())), preferred_element_type=F32)


def tiles(width):
    step = 512 if width % 512 == 0 else 256
    return [slice(at, at + step) for at in range(0, width, step)]


def columns(rows, width, index):
    return pl.BlockSpec((rows, width), lambda i: (0, index))


def cost(flops, size):
    return pl.CostEstimate(flops=flops, bytes_accessed=size, transcendentals=0)


def prepare_kernel(hidden, gain, routes, weights, out, sent):
    tokens, width = hidden.shape
    values = hidden[...].astype(F32)
    scale = lax.rsqrt(jnp.mean(values * values, axis=-1, keepdims=True) + 1e-06)
    out[:, :width] = (values * scale * gain[...].astype(F32)).astype(BF16)
    row = lax.broadcasted_iota(jnp.int32, (tokens, tokens), 0)
    col = lax.broadcasted_iota(jnp.int32, (tokens, tokens), 1)

    def upright(line):
        return jnp.sum(jnp.where(row == col, line.astype(F32), 0.0), axis=-1, keepdims=True)

    experts = [upright(routes[k:k + 1, :]) for k in range(2)]
    factors = [upright(weights[k:k + 1, :]) for k in range(2)]
    lane = lax.broadcasted_iota(jnp.int32, (tokens, INFO), 1)
    hits = [lane == e.astype(jnp.int32) for e in experts]
    named = (hits[0] | hits[1]).astype(F32).astype(BF16)
    earlier = dot((col < row).astype(F32).astype(BF16), named)
    info = jnp.zeros((tokens, INFO), F32)
    for k in range(2):
        slot = jnp.sum(jnp.where(hits[k], earlier, 0.0), axis=-1, keepdims=True)
        info = jnp.where(lane == k, experts[k], info)
        info = jnp.where(lane == 2 + k, slot, info)
        info = jnp.where(lane == 4 + k, factors[k], info)
    out[:, width:] = info.astype(BF16)
    sent[:, :SPLIT] = out[:, :SPLIT]
    sent[:, SPLIT:] = info.astype(BF16)


def prepare(hidden, gain, routes, weights):
    tokens, width = hidden.shape
    return pl.pallas_call(
        prepare_kernel,
        out_shape=[
            jax.ShapeDtypeStruct((tokens, width + INFO), BF16),
            jax.ShapeDtypeStruct((tokens, SPLIT + INFO), BF16),
        ],
        in_specs=[WHOLE] * 4,
        out_specs=[WHOLE] * 2,
        compiler_params=pltpu.CompilerParams(vmem_limit_bytes=16 * 1024 * 1024),
        cost_estimate=cost(0, 4 * tokens * width),
    )(hidden, gain.reshape(1, -1), routes.T, weights.T)


def places(info, side, core):
    info = info.astype(F32)
    row = lax.broadcasted_iota(jnp.int32, (info.shape[0], ROWS), 1)
    held = jnp.zeros(row.shape, F32)
    weight = jnp.zeros(row.shape, F32)
    for k in range(2):
        expert = info[:, k:k + 1].astype(jnp.int32)
        slot = info[:, 2 + k:3 + k].astype(jnp.int32)
        target = (expert >> 1) * (CORES * CAP) + side * CAP + slot
        target = jnp.where((expert & 1) == core, target, -1)
        held = jnp.where(row == target, 1.0, held)
        weight = jnp.where(row == target, info[:, 4 + k:5 + k], weight)
    return held.astype(BF16), weight.astype(BF16)


def gather_kernel(n_groups, first, cuts, core, *refs):
    outs = refs[2 * n_groups:]
    width = sum(cuts)
    at = 0
    for g in range(n_groups):
        mine, theirs = refs[2 * g:2 * g + 2]
        last = mine.shape[1] - INFO
        picks = [places(a[:, last:], side, core[0])[0] for side, a in enumerate((mine, theirs))]
        begin = first
        for i, cut in enumerate(cuts):
            for part in tiles(cut):
                source = slice(begin + part.start, begin + part.stop)
                rows = dot_t(picks[0], mine[:, source]) + dot_t(picks[1], theirs[:, source])
                out = outs[i]
                out[:, g * cut + part.start:g * cut + part.stop] = rows.astype(BF16)
            begin += cut


def gather(core, groups, first, cuts):
    flat = [a for pair in groups for a in pair]
    n_groups = len(groups)
    return pl.pallas_call(
        functools.partial(gather_kernel, n_groups, first, cuts),
        out_shape=[jax.ShapeDtypeStruct((ROWS, cut * n_groups), BF16) for cut in cuts],
        in_specs=[SCALAR] + [WHOLE] * len(flat),
        out_specs=[WHOLE] * len(cuts),
        compiler_params=pltpu.CompilerParams(vmem_limit_bytes=24 * 1024 * 1024),
        cost_estimate=cost(0, n_groups * ROWS * sum(cuts) * 4),
    )(core, *flat)


def mix_kernel(n_groups, core, *refs):
    back, mine_out, theirs_out = refs[2 * n_groups:]
    width = back.shape[1] // n_groups
    for g in range(n_groups):
        for side, out in enumerate((mine_out, theirs_out)):
            info = refs[2 * g + side]
            tokens = info.shape[0]
            weight = places(info[...], side, core[0])[1]
            for part in tiles(width):
                source = slice(g * width + part.start, g * width + part.stop)
                out[g * tokens:(g + 1) * tokens, part] = dot(weight, back[:, source]).astype(out.dtype)


def mix(core, groups, back):
    n_groups = len(groups)
    tokens = groups[0][0].shape[0]
    width = back.shape[1] // n_groups
    flat = [a for pair in groups for a in pair]
    specs = [columns(tokens, INFO, a.shape[1] // INFO - 1) for a in flat]
    return pl.pallas_call(
        functools.partial(mix_kernel, n_groups),
        out_shape=[
            jax.ShapeDtypeStruct((n_groups * tokens, width), F32),
            jax.ShapeDtypeStruct((n_groups * tokens, width), BF16),
        ],
        grid=(1,),
        in_specs=[SCALAR] + specs + [WHOLE],
        out_specs=[WHOLE] * 2,
        compiler_params=pltpu.CompilerParams(vmem_limit_bytes=24 * 1024 * 1024),
        cost_estimate=cost(0, ROWS * back.shape[1] * 4),
    )(core, *flat, back)


def expert_kernel(index, carried, n_out, *refs):
    early_hbm, low, high, gate_hbm, up_hbm, down_hbm = refs[:6]
    refs = refs[6:]
    if carried:
        carry, refs = refs[0], refs[1:]
    outs = refs[:n_out]
    gate_w, up_w, down_w, units, gate_sum, up_sum, early, sems = refs[n_out:]
    depth = early.shape[1]
    early_copy = pltpu.make_async_copy(
        early_hbm.at[:, pl.ds(index * depth, depth)], early, sems.at[5]
    )
    early_copy.start()
    copies = []
    for i, part in enumerate((pl.ds(0, depth), pl.ds(depth, gate_w.shape[0] - depth))):
        copies.append((
            pltpu.make_async_copy(gate_hbm.at[0, part], gate_w.at[part], sems.at[2 * i]),
            pltpu.make_async_copy(up_hbm.at[0, part], up_w.at[part], sems.at[2 * i + 1]),
        ))
    down_copy = pltpu.make_async_copy(down_hbm.at[0], down_w, sems.at[4])
    for pair in copies:
        for copy in pair:
            copy.start()
    down_copy.start()
    if carried:
        outs[0][:, :depth] = carry[...]
    early_copy.wait()
    for copy in copies[0]:
        copy.wait()
    for at in range(0, units.shape[1], TILE):
        cols = slice(at, at + TILE)
        gate_sum[:, cols] = dot(early[...], gate_w[:depth, cols])
        up_sum[:, cols] = dot(early[...], up_w[:depth, cols])
    for copy in copies[1]:
        copy.wait()
    middle = depth + low.shape[1]
    for at in range(0, units.shape[1], TILE):
        cols = slice(at, at + TILE)
        gate = dot(low[...], gate_w[depth:middle, cols]) + dot(high[...], gate_w[middle:, cols])
        gate += gate_sum[:, cols]
        up = dot(low[...], up_w[depth:middle, cols]) + dot(high[...], up_w[middle:, cols])
        up += up_sum[:, cols]
        units[:, cols] = (gate / (1.0 + jnp.exp(-gate)) * up).astype(BF16)
    down_copy.wait()
    order = ((1, depth), (2, middle), (0, 0))
    for i, begin in order:
        skip = depth if carried and i == 0 else 0
        for at in range(0, outs[i].shape[1] - skip, TILE):
            cols = slice(begin + at, begin + at + TILE)
            outs[i][:, skip + at:skip + at + TILE] = dot(units[...], down_w[:, cols]).astype(BF16)


def expert(early, low, high, weights, carry=None):
    early, index = early
    rows = low.shape[0]
    width, hidden_units = weights[0].shape[1:]
    left = pl.BlockSpec(memory_space=pl.ANY)
    carries = [] if carry is None else [carry]
    cuts = (SPLIT * (1 + len(carries)), low.shape[1], high.shape[1])
    return pl.pallas_call(
        functools.partial(expert_kernel, index, bool(carries), len(cuts)),
        out_shape=[jax.ShapeDtypeStruct((rows, cut), BF16) for cut in cuts],
        in_specs=[left] + [WHOLE] * 2 + [left] * 3 + [WHOLE] * len(carries),
        out_specs=[WHOLE] * len(cuts),
        scratch_shapes=[
            pltpu.VMEM((width, hidden_units), BF16),
            pltpu.VMEM((width, hidden_units), BF16),
            pltpu.VMEM((hidden_units, width), BF16),
            pltpu.VMEM((rows, hidden_units), BF16),
            pltpu.VMEM((rows, hidden_units), F32),
            pltpu.VMEM((rows, hidden_units), F32),
            pltpu.VMEM((rows, SPLIT), BF16),
            pltpu.SemaphoreType.DMA((6,)),
        ],
        compiler_params=pltpu.CompilerParams(vmem_limit_bytes=44 * 1024 * 1024),
        cost_estimate=pl.CostEstimate(
            flops=12 * rows * width * hidden_units,
            bytes_accessed=6 * width * hidden_units + 4 * rows * width,
            transcendentals=rows * hidden_units,
        ),
    )(early, low, high, *weights, *carries)


def on_device(hidden, norm_gain, w_gate, w_up, w_down, routes, gate_weights):
    tokens_here, width = hidden.shape
    chips = EXPERTS // CORES
    n_grp = lax.axis_size("grp")
    core = lax.axis_index("loc") % CORES
    core = core.astype(jnp.int32).reshape(1)
    plane = [[CORES * i + c for i in range(chips)] for c in range(CORES)]
    weights = (w_gate, w_up, w_down)

    def swap(rows):
        return lax.ppermute(rows, "loc", [(i, i ^ 1) for i in range(EXPERTS)])

    def shift(rows, way):
        return lax.ppermute(rows, "grp", [(i, (i + way) % n_grp) for i in range(n_grp)])

    turn = [None]

    def after(rows, other):
        return rows if other is None else lax.optimization_barrier((rows, other))[0]

    def exchange(rows, *others):
        for other in others:
            rows = after(rows, other)
        blocks = after(rows, turn[0]).reshape(chips, rows.shape[0] // chips, -1)
        out = lax.all_to_all(blocks, "loc", 0, 0, tiled=True, axis_index_groups=plane)
        turn[0] = out
        return out.reshape(rows.shape)

    def b16(a):
        return a.astype(BF16)

    def f32(a):
        return a.astype(F32)

    own, sent = prepare(hidden, norm_gain, routes, gate_weights)
    own_pair = (own, swap(own))
    near, next_, far = shift(sent, 1), shift(sent, -1), shift(sent, 2)
    low_rows, high_rows = gather(core, [own_pair], SPLIT, (HALF, width - SPLIT - HALF))

    low_own = exchange(low_rows, near, next_)
    low_near, low_next = shift(low_own, 1), shift(low_own, -1)
    near_pair = (near, swap(near))
    next_pair = (next_, swap(next_))
    far_pair = (far, swap(far))
    high_own = exchange(high_rows, far)
    high_near, high_next = shift(high_own, 1), shift(high_own, -1)
    low_far, high_far = shift(low_near, 1), shift(high_next, -1)
    rows = gather(core, [near_pair, next_pair], 0, (SPLIT,))[0]
    first_in = exchange(rows, low_near, low_next)
    rows = gather(core, [far_pair, own_pair], 0, (SPLIT,))[0]
    second_in = exchange(rows, high_near, high_next)

    out, near_low, near_high = expert((first_in, 0), low_near, high_near, weights)
    first_out, next_low, next_high = expert((first_in, 1), low_next, high_next, weights, out)
    near_high, next_low = shift(near_high, -1), shift(next_low, 1)
    first_back = exchange(first_out)
    far_out, far_low, far_high = expert((second_in, 0), low_far, high_far, weights)
    far_low, far_high = shift(far_low, -1), shift(far_high, 1)
    far_back = exchange(far_out)
    near_low = b16(f32(near_low) + f32(far_low))
    next_high = b16(f32(next_high) + f32(far_high))
    own_rows = after(after(low_own, near_high), next_low)
    own_out, own_low, own_high = expert((second_in, 1), own_rows, high_own, weights)
    own_back = exchange(own_out, far_low, far_high)
    low_sum = b16(f32(own_low) + f32(next_low) + f32(shift(near_low, -1)))
    high_sum = b16(f32(own_high) + f32(near_high) + f32(shift(next_high, 1)))
    late_back = exchange(jnp.concatenate([low_sum, high_sum], axis=1))

    mine, theirs = mix(core, [near_pair, next_pair], first_back)
    mine = b16(mine + f32(swap(theirs)))
    total = f32(shift(mine[:tokens_here], -1)) + f32(shift(mine[tokens_here:], 1))
    mine, theirs = mix(core, [far_pair], far_back)
    total += f32(shift(b16(mine + f32(swap(theirs))), 2))
    mine, theirs = mix(core, [own_pair], own_back)
    total += mine + f32(swap(theirs))
    mine, theirs = mix(core, [own_pair], late_back)
    late = b16(mine + f32(swap(theirs)))
    return jnp.concatenate([b16(total), late], axis=1)


def solution(mesh):
    placed = (
        P(("grp", "loc"), None),
        P(),
        P("loc", None, "grp"),
        P("loc", None, "grp"),
        P("loc", "grp", None),
        P(("grp", "loc"), None),
        P(("grp", "loc"), None),
    )
    return jax.shard_map(
        on_device, mesh=mesh, in_specs=placed, out_specs=P(("grp", "loc"), None), check_vma=False
    )
```

```python
import functools
import jax
import jax.numpy as jnp
from jax import lax
from jax.experimental import pallas as pl
from jax.experimental.pallas import tpu as pltpu
from jax.sharding import PartitionSpec as P

EXPERTS = 32
CAP = 12
CORES = 2
INFO = 128
SPLIT = 1536
HALF = 1280
TILE = 256


BF16 = jnp.bfloat16
F32 = jnp.float32
ROWS = EXPERTS * CAP
WHOLE = pl.BlockSpec(memory_space=pltpu.VMEM)
SCALAR = pl.BlockSpec(memory_space=pltpu.SMEM)


def dot(a, b):
    return jnp.dot(a, b, preferred_element_type=F32)


def dot_t(a, b):
    return lax.dot_general(a, b, (((0,), (0,)), ((), ())), preferred_element_type=F32)


def tiles(width):
    step = 512 if width % 512 == 0 else 256
    return [slice(at, at + step) for at in range(0, width, step)]


def columns(rows, width, index):
    return pl.BlockSpec((rows, width), lambda i: (0, index))


def cost(flops, size):
    return pl.CostEstimate(flops=flops, bytes_accessed=size, transcendentals=0)


def prepare_kernel(hidden, gain, routes, weights, out, sent):
    tokens, width = hidden.shape
    values = hidden[...].astype(F32)
    scale = lax.rsqrt(jnp.mean(values * values, axis=-1, keepdims=True) + 1e-06)
    out[:, :width] = (values * scale * gain[...].astype(F32)).astype(BF16)
    row = lax.broadcasted_iota(jnp.int32, (tokens, tokens), 0)
    col = lax.broadcasted_iota(jnp.int32, (tokens, tokens), 1)

    def upright(line):
        return jnp.sum(jnp.where(row == col, line.astype(F32), 0.0), axis=-1, keepdims=True)

    experts = [upright(routes[k:k + 1, :]) for k in range(2)]
    factors = [upright(weights[k:k + 1, :]) for k in range(2)]
    lane = lax.broadcasted_iota(jnp.int32, (tokens, INFO), 1)
    hits = [lane == e.astype(jnp.int32) for e in experts]
    named = (hits[0] | hits[1]).astype(F32).astype(BF16)
    earlier = dot((col < row).astype(F32).astype(BF16), named)
    info = jnp.zeros((tokens, INFO), F32)
    for k in range(2):
        slot = jnp.sum(jnp.where(hits[k], earlier, 0.0), axis=-1, keepdims=True)
        info = jnp.where(lane == k, experts[k], info)
        info = jnp.where(lane == 2 + k, slot, info)
        info = jnp.where(lane == 4 + k, factors[k], info)
    out[:, width:] = info.astype(BF16)
    sent[:, :SPLIT] = out[:, :SPLIT]
    sent[:, SPLIT:] = info.astype(BF16)


def prepare(hidden, gain, routes, weights):
    tokens, width = hidden.shape
    return pl.pallas_call(
        prepare_kernel,
        out_shape=[
            jax.ShapeDtypeStruct((tokens, width + INFO), BF16),
            jax.ShapeDtypeStruct((tokens, SPLIT + INFO), BF16),
        ],
        in_specs=[WHOLE] * 4,
        out_specs=[WHOLE] * 2,
        compiler_params=pltpu.CompilerParams(vmem_limit_bytes=16 * 1024 * 1024),
        cost_estimate=cost(0, 4 * tokens * width),
    )(hidden, gain.reshape(1, -1), routes.T, weights.T)


def places(info, side, core):
    info = info.astype(F32)
    row = lax.broadcasted_iota(jnp.int32, (info.shape[0], ROWS), 1)
    held = jnp.zeros(row.shape, F32)
    weight = jnp.zeros(row.shape, F32)
    for k in range(2):
        expert = info[:, k:k + 1].astype(jnp.int32)
        slot = info[:, 2 + k:3 + k].astype(jnp.int32)
        target = (expert >> 1) * (CORES * CAP) + side * CAP + slot
        target = jnp.where((expert & 1) == core, target, -1)
        held = jnp.where(row == target, 1.0, held)
        weight = jnp.where(row == target, info[:, 4 + k:5 + k], weight)
    return held.astype(BF16), weight.astype(BF16)


def gather_kernel(n_groups, first, cuts, core, *refs):
    outs = refs[2 * n_groups:]
    width = sum(cuts)
    at = 0
    for g in range(n_groups):
        mine, theirs = refs[2 * g:2 * g + 2]
        last = mine.shape[1] - INFO
        picks = [places(a[:, last:], side, core[0])[0] for side, a in enumerate((mine, theirs))]
        begin = first
        for i, cut in enumerate(cuts):
            for part in tiles(cut):
                source = slice(begin + part.start, begin + part.stop)
                rows = dot_t(picks[0], mine[:, source]) + dot_t(picks[1], theirs[:, source])
                out = outs[i]
                out[:, g * cut + part.start:g * cut + part.stop] = rows.astype(BF16)
            begin += cut


def gather(core, groups, first, cuts):
    flat = [a for pair in groups for a in pair]
    n_groups = len(groups)
    return pl.pallas_call(
        functools.partial(gather_kernel, n_groups, first, cuts),
        out_shape=[jax.ShapeDtypeStruct((ROWS, cut * n_groups), BF16) for cut in cuts],
        in_specs=[SCALAR] + [WHOLE] * len(flat),
        out_specs=[WHOLE] * len(cuts),
        compiler_params=pltpu.CompilerParams(vmem_limit_bytes=24 * 1024 * 1024),
        cost_estimate=cost(0, n_groups * ROWS * sum(cuts) * 4),
    )(core, *flat)


def mix_kernel(n_groups, core, *refs):
    back, mine_out, theirs_out = refs[2 * n_groups:]
    width = back.shape[1] // n_groups
    for g in range(n_groups):
        for side, out in enumerate((mine_out, theirs_out)):
            info = refs[2 * g + side]
            tokens = info.shape[0]
            weight = places(info[...], side, core[0])[1]
            for part in tiles(width):
                source = slice(g * width + part.start, g * width + part.stop)
                out[g * tokens:(g + 1) * tokens, part] = dot(weight, back[:, source]).astype(out.dtype)


def mix(core, groups, back):
    n_groups = len(groups)
    tokens = groups[0][0].shape[0]
    width = back.shape[1] // n_groups
    flat = [a for pair in groups for a in pair]
    specs = [columns(tokens, INFO, a.shape[1] // INFO - 1) for a in flat]
    return pl.pallas_call(
        functools.partial(mix_kernel, n_groups),
        out_shape=[
            jax.ShapeDtypeStruct((n_groups * tokens, width), F32),
            jax.ShapeDtypeStruct((n_groups * tokens, width), BF16),
        ],
        grid=(1,),
        in_specs=[SCALAR] + specs + [WHOLE],
        out_specs=[WHOLE] * 2,
        compiler_params=pltpu.CompilerParams(vmem_limit_bytes=24 * 1024 * 1024),
        cost_estimate=cost(0, ROWS * back.shape[1] * 4),
    )(core, *flat, back)


def expert_kernel(index, carried, n_out, *refs):
    early_hbm, low, high, gate_hbm, up_hbm, down_hbm = refs[:6]
    refs = refs[6:]
    if carried:
        carry, refs = refs[0], refs[1:]
    outs = refs[:n_out]
    gate_w, up_w, down_w, units, gate_sum, up_sum, early, sems = refs[n_out:]
    depth = early.shape[1]
    early_copy = pltpu.make_async_copy(
        early_hbm.at[:, pl.ds(index * depth, depth)], early, sems.at[5]
    )
    early_copy.start()
    copies = []
    for i, part in enumerate((pl.ds(0, depth), pl.ds(depth, gate_w.shape[0] - depth))):
        copies.append((
            pltpu.make_async_copy(gate_hbm.at[0, part], gate_w.at[part], sems.at[2 * i]),
            pltpu.make_async_copy(up_hbm.at[0, part], up_w.at[part], sems.at[2 * i + 1]),
        ))
    down_copy = pltpu.make_async_copy(down_hbm.at[0], down_w, sems.at[4])
    for pair in copies:
        for copy in pair:
            copy.start()
    down_copy.start()
    if carried:
        outs[0][:, :depth] = carry[...]
    early_copy.wait()
    for copy in copies[0]:
        copy.wait()
    for at in range(0, units.shape[1], TILE):
        cols = slice(at, at + TILE)
        gate_sum[:, cols] = dot(early[...], gate_w[:depth, cols])
        up_sum[:, cols] = dot(early[...], up_w[:depth, cols])
    for copy in copies[1]:
        copy.wait()
    middle = depth + low.shape[1]
    for at in range(0, units.shape[1], TILE):
        cols = slice(at, at + TILE)
        gate = dot(low[...], gate_w[depth:middle, cols]) + dot(high[...], gate_w[middle:, cols])
        gate += gate_sum[:, cols]
        up = dot(low[...], up_w[depth:middle, cols]) + dot(high[...], up_w[middle:, cols])
        up += up_sum[:, cols]
        units[:, cols] = (gate / (1.0 + jnp.exp(-gate)) * up).astype(BF16)
    down_copy.wait()
    order = ((1, depth), (2, middle), (0, 0))
    for i, begin in order:
        skip = depth if carried and i == 0 else 0
        for at in range(0, outs[i].shape[1] - skip, TILE):
            cols = slice(begin + at, begin + at + TILE)
            outs[i][:, skip + at:skip + at + TILE] = dot(units[...], down_w[:, cols]).astype(BF16)


def expert(early, low, high, weights, carry=None):
    early, index = early
    rows = low.shape[0]
    width, hidden_units = weights[0].shape[1:]
    left = pl.BlockSpec(memory_space=pl.ANY)
    carries = [] if carry is None else [carry]
    cuts = (SPLIT * (1 + len(carries)), low.shape[1], high.shape[1])
    return pl.pallas_call(
        functools.partial(expert_kernel, index, bool(carries), len(cuts)),
        out_shape=[jax.ShapeDtypeStruct((rows, cut), BF16) for cut in cuts],
        in_specs=[left] + [WHOLE] * 2 + [left] * 3 + [WHOLE] * len(carries),
        out_specs=[WHOLE] * len(cuts),
        scratch_shapes=[
            pltpu.VMEM((width, hidden_units), BF16),
            pltpu.VMEM((width, hidden_units), BF16),
            pltpu.VMEM((hidden_units, width), BF16),
            pltpu.VMEM((rows, hidden_units), BF16),
            pltpu.VMEM((rows, hidden_units), F32),
            pltpu.VMEM((rows, hidden_units), F32),
            pltpu.VMEM((rows, SPLIT), BF16),
            pltpu.SemaphoreType.DMA((6,)),
        ],
        compiler_params=pltpu.CompilerParams(vmem_limit_bytes=44 * 1024 * 1024),
        cost_estimate=pl.CostEstimate(
            flops=12 * rows * width * hidden_units,
            bytes_accessed=6 * width * hidden_units + 4 * rows * width,
            transcendentals=rows * hidden_units,
        ),
    )(early, low, high, *weights, *carries)


def on_device(hidden, norm_gain, w_gate, w_up, w_down, routes, gate_weights):
    tokens_here, width = hidden.shape
    chips = EXPERTS // CORES
    n_grp = lax.axis_size("grp")
    core = lax.axis_index("loc") % CORES
    core = core.astype(jnp.int32).reshape(1)
    plane = [[CORES * i + c for i in range(chips)] for c in range(CORES)]
    weights = (w_gate, w_up, w_down)

    def swap(rows):
        return lax.ppermute(rows, "loc", [(i, i ^ 1) for i in range(EXPERTS)])

    def shift(rows, way):
        return lax.ppermute(rows, "grp", [(i, (i + way) % n_grp) for i in range(n_grp)])

    turn = [None]

    def after(rows, other):
        return rows if other is None else lax.optimization_barrier((rows, other))[0]

    def exchange(rows, *others):
        for other in others:
            rows = after(rows, other)
        blocks = after(rows, turn[0]).reshape(chips, rows.shape[0] // chips, -1)
        out = lax.all_to_all(blocks, "loc", 0, 0, tiled=True, axis_index_groups=plane)
        turn[0] = out
        return out.reshape(rows.shape)

    def b16(a):
        return a.astype(BF16)

    def f32(a):
        return a.astype(F32)

    own, sent = prepare(hidden, norm_gain, routes, gate_weights)
    own_pair = (own, swap(own))
    near, next_, far = shift(sent, 1), shift(sent, -1), shift(sent, 2)
    low_rows, high_rows = gather(core, [own_pair], SPLIT, (HALF, width - SPLIT - HALF))

    low_own = exchange(low_rows, near, next_)
    low_near, low_next = shift(low_own, 1), shift(low_own, -1)
    near_pair = (near, swap(near))
    next_pair = (next_, swap(next_))
    far_pair = (far, swap(far))
    high_own = exchange(high_rows, far)
    high_near, high_next = shift(high_own, 1), shift(high_own, -1)
    low_far, high_far = shift(low_near, 1), shift(high_next, -1)
    rows = gather(core, [near_pair, next_pair], 0, (SPLIT,))[0]
    first_in = exchange(rows, low_near, low_next)
    rows = gather(core, [far_pair, own_pair], 0, (SPLIT,))[0]
    second_in = exchange(rows, high_near, high_next)

    out, near_low, near_high = expert((first_in, 0), low_near, high_near, weights)
    first_out, next_low, next_high = expert((first_in, 1), low_next, high_next, weights, out)
    near_high, next_low = shift(near_high, -1), shift(next_low, 1)
    first_back = exchange(first_out, low_far, high_far)
    far_out, far_low, far_high = expert((second_in, 0), low_far, high_far, weights)
    far_low, far_high = shift(far_low, -1), shift(far_high, 1)
    far_back = exchange(far_out, near_high, next_low)
    own_out, own_low, own_high = expert((second_in, 1), low_own, high_own, weights)
    near_low = b16(f32(near_low) + f32(after(far_low, own_out)))
    next_high = b16(f32(next_high) + f32(after(far_high, own_out)))
    mine, theirs = mix(core, [near_pair, next_pair], first_back)
    theirs = swap(theirs)
    own_back = exchange(own_out, far_low, far_high, theirs)
    low_sum = b16(f32(own_low) + f32(next_low) + f32(shift(near_low, -1)))
    high_sum = b16(f32(own_high) + f32(near_high) + f32(shift(next_high, 1)))
    late_back = exchange(jnp.concatenate([low_sum, high_sum], axis=1))

    mine = b16(mine + f32(theirs))
    total = f32(shift(mine[:tokens_here], -1)) + f32(shift(mine[tokens_here:], 1))
    mine, theirs = mix(core, [far_pair], far_back)
    total += f32(shift(b16(mine + f32(swap(theirs))), 2))
    mine, theirs = mix(core, [own_pair], own_back)
    total += mine + f32(swap(theirs))
    mine, theirs = mix(core, [own_pair], late_back)
    late = b16(mine + f32(swap(theirs)))
    return jnp.concatenate([b16(total), late], axis=1)


def solution(mesh):
    placed = (
        P(("grp", "loc"), None),
        P(),
        P("loc", None, "grp"),
        P("loc", None, "grp"),
        P("loc", "grp", None),
        P(("grp", "loc"), None),
        P(("grp", "loc"), None),
    )
    return jax.shard_map(
        on_device, mesh=mesh, in_specs=placed, out_specs=P(("grp", "loc"), None), check_vma=False
    )
```
